32 devices in a mesh: prow: 4 (over y, x), pcol: 8 (over z, core).
Axes of the slice: x: 2, y: 2, z: 4, core: 2. Of those that a mesh axis runs over, the one named last changes fastest.
Arguments:
- left_factor: bfloat16 [16, 16, 2048, 128], P('prow', 'pcol'), may hold values from -0.8984375 to 0.8984375
- right_factor: bfloat16 [16, 16, 2048, 128], P('prow', 'pcol'), may hold values from -0.8984375 to 0.8984375
- pivot_left: bfloat16 [16, 2048, 128], P('pcol', 'prow'), may hold values from -0.8984375 to 0.8984375
- pivot_right: bfloat16 [16, 2048, 128], P('pcol', 'prow'), may hold values from -0.8984375 to 0.8984375
- target_left: bfloat16 [2048, 16, 128], P('pcol', 'prow'), may hold values from -6 to 6
- target_right: bfloat16 [2048, 16, 128], P('pcol', 'prow'), may hold values from -6 to 6
- probe: bfloat16 [2048, 128], P('prow'), may hold values from -6 to 6
- ranks: int32 [16, 16], P('prow', 'pcol'), may hold values from 16 to 128
Outputs:
- basis: float32 [2048, 16, 128], P('pcol', 'prow')
- coefficient: float32 [2048, 16, 128], P('pcol', 'prow')
The draws below stay inside these ranges and needn't reach their ends.
All inputs are finite; a program needn't handle non-finite values.
Results may differ from the reference program's by a relative error of at most 0.0038.
Values may be sent and summed in bfloat16 or wider, within the bound.
A program may use at most 64 MiB of HBM per device.

```python
from functools import partial
import jax
import jax.numpy as jnp
from jax import lax

B = 2048
R = 128
NT = 16
NC = 16


def with_ends(values, stream_key, least, top_value):
    index_at = [jax.random.randint(jax.random.fold_in(stream_key, axis), (), 0, length) for axis, length in enumerate(values.shape)]
    widest = values.shape.index(max(values.shape))
    beside = index_at[:widest] + [(index_at[widest] + 1) % values.shape[widest]] + index_at[widest + 1:]
    return values.at[tuple(index_at)].set(least).at[tuple(beside)].set(top_value)


def block_scale(stream_key, extent, shards, least, largest):
    loudness = 1.0
    for position, parts in shards:
        heights = jax.random.uniform(jax.random.fold_in(jax.random.fold_in(stream_key, 6), position), (parts,), jnp.float32, least / len(shards), largest / len(shards))
        loudness = loudness * jnp.repeat(jnp.exp(heights), extent[position] // parts).reshape((-1,) + (1,) * (len(extent) - 1 - position))
    return loudness


def scatter_about(stream_key, extent, deviation, bound, pieces=(), dtype=jnp.bfloat16):
    array = deviation * jax.random.normal(stream_key, extent, jnp.float32)
    if pieces:
        array = array * block_scale(stream_key, extent, pieces, -0.22, 0.18)
    return jnp.clip(array, -bound, bound).astype(dtype)


def setup_inputs(seed: int = 0) -> dict:
    arg_keys = jax.random.split(jax.random.key(seed), 9)
    return {
        "left_factor": scatter_about(arg_keys[0], (NT, NC, B, R), 0.15, 0.8984375, ((0, 4), (1, 8))),
        "right_factor": scatter_about(arg_keys[1], (NT, NC, B, R), 0.15, 0.8984375, ((0, 4), (1, 8))),
        "pivot_left": scatter_about(arg_keys[2], (NC, B, R), 0.15, 0.8984375, ((0, 8), (1, 4))),
        "pivot_right": scatter_about(arg_keys[3], (NC, B, R), 0.15, 0.8984375, ((0, 8), (1, 4))),
        "target_left": scatter_about(arg_keys[4], (B, NT, R), 1.0, 6.0, ((0, 8), (1, 4))),
        "target_right": scatter_about(arg_keys[5], (B, NT, R), 1.0, 6.0, ((0, 8), (1, 4))),
        "probe": scatter_about(arg_keys[6], (B, R), 1.0, 6.0, ((0, 4),)),
        "ranks": with_ends(jax.random.randint(arg_keys[7], (NT, NC), R // 8, R + 1), jax.random.fold_in(arg_keys[7], 1), R // 8, R).astype(jnp.int32),
    }


exact_mode = lax.Precision.HIGHEST

def one_target(pivot_sample, pivot_left, pivot_right, target_items):
    left_tile, right_tile, tile_ranks, plain_left, plain_right, target_sample = target_items
    rank_mask = (jnp.arange(R)[None, :] < tile_ranks[:, None]).astype(jnp.float32)
    coupling = jnp.einsum('jbr,jbs->jrs', right_tile.astype(jnp.float32), pivot_right.astype(jnp.float32))
    coupling = coupling * rank_mask[:, :, None]
    weights = jnp.einsum('jrs,jst->jrt', coupling, pivot_sample, precision=exact_mode).astype(jnp.bfloat16)
    direct = jnp.einsum('bs,st->bt', plain_left.astype(jnp.float32), target_sample, precision=exact_mode)
    update = jnp.einsum('jbr,jrt->bt', left_tile.astype(jnp.float32), weights.astype(jnp.float32))
    samples = direct - update
    gram_matrix = jnp.dot(samples.T, samples, precision=exact_mode) / B
    lower_factor = jnp.linalg.cholesky(gram_matrix)
    basis_tile = lax.linalg.triangular_solve(lower_factor, samples, left_side=False, lower=True, transpose_a=True)
    basis_half = basis_tile.astype(jnp.bfloat16)
    correlation = jnp.einsum('jbr,bt->jrt', left_tile.astype(jnp.float32), basis_half.astype(jnp.float32))
    reduced = jnp.einsum('jrs,jrt->jst', coupling, correlation, precision=exact_mode).astype(jnp.bfloat16)
    target_correlation = jnp.einsum('bs,bt->st', plain_left.astype(jnp.float32), basis_half.astype(jnp.float32)).astype(jnp.bfloat16)
    own_term = jnp.einsum('bs,st->bt', plain_right.astype(jnp.float32), target_correlation.astype(jnp.float32))
    pivot_term = jnp.einsum('jbs,jst->bt', pivot_left.astype(jnp.float32), reduced.astype(jnp.float32))
    coefficient = (own_term - pivot_term) / B
    return (basis_tile, coefficient)

def reference(left_factor, right_factor, pivot_left, pivot_right, target_left, target_right, probe, ranks):
    probe_wide = probe.astype(jnp.float32)
    pivot_sample = jnp.einsum('jbr,bs->jrs', pivot_left.astype(jnp.float32), probe_wide)
    target_sample = jnp.einsum('bir,bs->irs', target_right.astype(jnp.float32), probe_wide)
    target_items = (left_factor, right_factor, ranks, jnp.transpose(target_left, (1, 0, 2)), jnp.transpose(target_right, (1, 0, 2)), target_sample)
    basis_all, coefficient_all = lax.map(partial(one_target, pivot_sample, pivot_left, pivot_right), target_items)
    return (jnp.transpose(basis_all, (1, 0, 2)), jnp.transpose(coefficient_all, (1, 0, 2)))
```

```python
import functools

import jax
import jax.numpy as jnp
from jax import lax
from jax.experimental import pallas as pl
from jax.experimental.pallas import tpu as pltpu
from jax.sharding import PartitionSpec as P

EXACT = lax.Precision.HIGHEST
MESH = pl.DeviceIdType.MESH
F32 = jnp.float32
BF16 = jnp.bfloat16


def dot(a, b, ca, cb, precision=None):
    return lax.dot_general(
        a, b, (((ca,), (cb,)), ((), ())), precision=precision, preferred_element_type=F32
    )


def inverse_factor(gram_ref, eye_ref, out_ref, start, tiles, span, block):
    row_in_block = lax.broadcasted_iota(jnp.int32, (tiles, block, 1), 1)
    rows = lax.broadcasted_iota(jnp.int32, (tiles, span, span), 1)
    columns = lax.broadcasted_iota(jnp.int32, (tiles, span, span), 2)
    group = slice(start, start + tiles)
    eye_ref[group] = (rows == columns).astype(F32)
    for first in range(0, span, block):
        g = gram_ref[group, first : first + block, :]
        e = eye_ref[group, first : first + block, :]
        for k in range(block):
            column = jnp.broadcast_to(
                g[:, :, first + k : first + k + 1], (tiles, block, span)
            )
            pivot = column[:, k : k + 1, :]
            scale = lax.rsqrt(pivot)
            scale = scale * (1.5 - 0.5 * pivot * scale * scale)
            g_row = g[:, k : k + 1, :] * scale
            e_row = e[:, k : k + 1, :] * scale
            factor = column * scale
            below = row_in_block > k
            here = row_in_block == k
            g = jnp.where(below, g - factor * g_row, jnp.where(here, g_row, g))
            e = jnp.where(below, e - factor * e_row, jnp.where(here, e_row, e))
        out_ref[group, first : first + block, :] = e
        if first + block < span:
            for i in range(tiles):
                gi, ei = g[i], e[i]
                turned = gi.T
                gram_ref[start + i] = gram_ref[start + i] - dot(turned, gi, 1, 0, EXACT)
                eye_ref[start + i] = eye_ref[start + i] - dot(turned, ei, 1, 0, EXACT)


def kernel(
    n_p, n_q,
    left_hbm, right_hbm, pivot_left, pivot_right, target_left, target_right, probe, ranks_hbm,
    basis, coefficient,
    ranks, left, right, left_full, right_full, probe_block, coupling, weights,
    ps_part, ps_recv, ps_sum,
    t_part, t_sib, t_chip, t_z, t_own, t_other, t_full,
    acc, sib_send, sib_recv, z_send, z_recv,
    samples, samples_full, raw,
    c_part, c_sib, c_chip, c_z, c_own, c_other, c_full,
    gram, eye, inverse, reduced,
    sib_send2, sib_recv2, z_send2, z_recv2,
    local_sem, probe_s, probe_r, pr_s, pr_r, ps_s, ps_r, pl_s, pl_r,
    ts_s, ts_r, tz_s, tz_r, to_s, to_r,
    ss_s, ss_r, sz_s, sz_r,
    gz_s, gz_r, gs_s, gs_r,
    cs_s, cs_r, cz_s, cz_r, co_s, co_r,
    fs_s, fs_r, fz_s, fz_r,
):
    p = lax.axis_index("prow")
    q = lax.axis_index("pcol")
    n_z = n_q // 2
    z = q // 2
    c = q % 2
    sibling = (p, q + 1 - 2 * c)
    ni, nj, order, span = left.shape
    rp = probe.shape[0]
    rq = target_left.shape[1]
    half = ni // 2

    def peer_p(d):
        return (lax.rem(p + d, n_p), q)

    def peer_z(d):
        return (p, lax.rem(z + d, n_z) * 2 + c)

    def row_block(index, size):
        return pl.ds(pl.multiple_of(index * size, size), size)

    def remote(src, dst, s, r, where):
        return pltpu.make_async_remote_copy(
            src_ref=src, dst_ref=dst, send_sem=s, recv_sem=r, device_id=where, device_id_type=MESH
        )

    right_copy = pltpu.make_async_copy(right_hbm, right, local_sem.at[0])
    left_copy = pltpu.make_async_copy(left_hbm, left, local_sem.at[1])
    right_copy.start()
    left_copy.start()
    ranks_copy = pltpu.make_async_copy(ranks_hbm, ranks, local_sem.at[2])
    ranks_copy.start()

    barrier = pltpu.get_barrier_semaphore()
    partners = [peer_p(d) for d in range(1, n_p)] + [peer_z(d) for d in range(1, n_z)] + [sibling]
    for partner in partners:
        pl.semaphore_signal(barrier, inc=1, device_id=partner, device_id_type=MESH)
    pl.semaphore_wait(barrier, len(partners))

    owner = (q * rq) // rp

    def mine():
        return pl.ds(pl.multiple_of(lax.rem(q * rq, rp), rq), rq)

    @pl.when(p == owner)
    def _():
        for d in range(1, n_p):
            remote(probe.at[mine()], probe_block, probe_s.at[d - 1], probe_r, peer_p(d)).start()
        probe_block[...] = probe[mine(), :]

    pr_copies = [
        remote(pivot_right, right_full.at[:, row_block(p, rp), :], pr_s.at[d - 1], pr_r.at[d - 1], peer_p(d))
        for d in range(1, n_p)
    ]
    for copy in pr_copies:
        copy.start()
    for j in range(nj):
        ps_part[j] = dot(pivot_left[j], probe[...], 0, 0)
    ps_copies = [
        remote(ps_part, ps_recv.at[d - 1], ps_s.at[d - 1], ps_r.at[d - 1], peer_p(d))
        for d in range(1, n_p)
    ]
    for copy in ps_copies:
        copy.start()
    pl_copies = [
        remote(pivot_left, left_full.at[:, row_block(p, rp), :], pl_s.at[d - 1], pl_r.at[d - 1], peer_p(d))
        for d in range(1, n_p)
    ]
    @pl.when(p != owner)
    def _():
        remote(probe.at[mine()], probe_block, probe_s.at[0], probe_r, peer_p(1)).wait_recv()

    for i in range(ni):
        t_part[i] = dot(target_right[i], probe_block[...], 0, 0)

    def half_of(core):
        return pl.ds(core * half, half)

    t_first = remote(t_part.at[half_of(1 - c)], t_sib, ts_s, ts_r, sibling)
    t_first.start()
    right_copy.wait()

    def couple(rows, chunk_ref):
        def body(n, carry):
            i, j = n // nj, n % nj
            coupling[i, j] += dot(chunk_ref[j], right[i, j, rows, :], 0, 0)
            return carry
        lax.fori_loop(0, ni * nj, body, 0)

    coupling[...] = jnp.zeros_like(coupling)
    couple(row_block(p, rp), pivot_right)

    t_first.wait()
    t_chip[...] = t_part[half_of(c)] + t_sib[...]
    t_second = [
        remote(t_chip, t_z.at[d - 1], tz_s.at[d - 1], tz_r.at[d - 1], peer_z(d)) for d in range(1, n_z)
    ]
    for copy in t_second:
        copy.start()

    for d in range(1, n_p):
        pr_copies[d - 1].wait()
        rows = row_block(lax.rem(p - d + n_p, n_p), rp)
        couple(rows, right_full.at[:, rows, :])
    total = ps_part[...]
    for d in range(1, n_p):
        ps_copies[d - 1].wait()
        total = total + ps_recv[d - 1]
    ps_sum[...] = total
    for copy in pl_copies:
        copy.start()
    left_copy.wait()
    ranks_copy.wait()

    sib_copies = lambda i: remote(sib_send.at[i], sib_recv.at[i], ss_s.at[i], ss_r.at[i], sibling)
    z_copies = lambda i, d: remote(
        z_send.at[i, d - 1], z_recv.at[i, d - 1], sz_s.at[i, d - 1], sz_r.at[i, d - 1], peer_z(d)
    )
    lane = lax.broadcasted_iota(jnp.int32, (span, span), 1)

    def update(i, carry):
        for j in range(nj):
            masked = jnp.where(lane < ranks[i, j], coupling[i, j], 0.0)
            coupling[i, j] = masked
            weights[j] = dot(masked.T, ps_sum[j], 1, 0, EXACT).astype(BF16)

        def rows_of(zz, inner):
            for parity in range(2):
                core = c if parity == 0 else 1 - c
                rows = row_block(2 * zz + core, rq)
                part = dot(left[i, 0, rows, :], weights[0], 1, 0)
                for j in range(1, nj):
                    part = part + dot(left[i, j, rows, :], weights[j], 1, 0)
                if parity == 0:
                    acc[i, zz] = part
                else:
                    sib_send[i, zz] = part.astype(BF16)
            return inner

        lax.fori_loop(0, n_z, rows_of, 0)
        sib_copies(i).start()
        return carry

    lax.fori_loop(0, ni, update, 0)

    def forward(i, carry):
        sib_copies(i).wait()
        for d in range(1, n_z):
            to = lax.rem(z + d, n_z)
            z_send[i, d - 1] = (acc[i, to] + sib_recv[i, to].astype(F32)).astype(BF16)
            z_copies(i, d).start()
        return carry

    def sent(i, carry):
        for d in range(1, n_z):
            z_copies(i, d).wait_send()
        return carry

    lax.fori_loop(0, half, forward, 0)

    def finish(second, chip, arrived, own, other, whole, s, r):
        for copy in second:
            copy.wait()
        value = chip[...].astype(F32)
        for d in range(1, n_z):
            value = value + arrived[d - 1].astype(F32)
        own[...] = value
        last = remote(own, other, s, r, sibling)
        last.start()
        last.wait()
        whole[half_of(c)] = own[...]
        whole[half_of(1 - c)] = other[...]

    finish(t_second, t_chip, t_z, t_own, t_other, t_full, to_s, to_r)
    lax.fori_loop(0, half, sent, 0)
    lax.fori_loop(half, ni, forward, 0)

    gather_z = lambda i, d: remote(
        samples_full.at[i, row_block(q, rq), :], samples_full.at[i, row_block(q, rq), :],
        gz_s.at[i, d - 1], gz_r.at[i, d - 1], peer_z(d),
    )

    def gather_sib(i, d):
        rows = row_block(2 * lax.rem(z - d + n_z, n_z) + c, rq)
        block = samples_full.at[i, rows, :]
        return remote(block, block, gs_s.at[i, d], gs_r.at[i, d], sibling)

    def sample(i, carry):
        value = dot(target_left[i].astype(F32), t_full[i], 1, 0, EXACT)
        value = value - acc[i, z] - sib_recv[i, z].astype(F32)
        for d in range(1, n_z):
            z_copies(i, d).wait_recv()
            value = value - z_recv[i, d - 1].astype(F32)
        samples[i] = value
        rounded = value.astype(BF16)
        samples_full[i, row_block(q, rq), :] = rounded
        for d in range(1, n_z):
            gather_z(i, d).start()
        gather_sib(i, 0).start()
        c_part[i] = dot(rounded, target_left[i], 0, 0)
        return carry

    lax.fori_loop(0, ni, sample, 0)
    lax.fori_loop(half, ni, sent, 0)
    c_first = remote(c_part.at[half_of(1 - c)], c_sib, cs_s, cs_r, sibling)
    c_first.start()

    def relay(i, carry):
        for d in range(1, n_z):
            gather_z(i, d).wait()
            gather_sib(i, d).start()
        return carry

    c_first.wait()
    c_chip[...] = (c_part[half_of(c)] + c_sib[...]).astype(BF16)
    c_second = [
        remote(c_chip, c_z.at[d - 1], cz_s.at[d - 1], cz_r.at[d - 1], peer_z(d)) for d in range(1, n_z)
    ]
    for copy in c_second:
        copy.start()

    def correlate(i, carry):
        for d in range(n_z):
            gather_sib(i, d).wait()
        turned = samples_full[i].T
        gram[i] = dot(turned, samples_full[i], 1, 0) * (1.0 / order)
        for j in range(nj):
            raw[i, j] = dot(turned, left[i, j], 1, 0)
        return carry

    sib_copies2 = lambda i: remote(sib_send2.at[i], sib_recv2.at[i], fs_s.at[i], fs_r.at[i], sibling)
    z_copies2 = lambda i, d: remote(
        z_send2.at[i, d - 1], z_recv2.at[i, d - 1], fz_s.at[i, d - 1], fz_r.at[i, d - 1], peer_z(d)
    )

    def project(i, carry):
        for j in range(nj):
            turned = dot(inverse[i], raw[i, j], 1, 0, EXACT)
            reduced[j] = dot(coupling[i, j], turned, 1, 1, EXACT).astype(BF16)

        def rows_of(zz, inner):
            for parity in range(2):
                core = c if parity == 0 else 1 - c
                rows = row_block(2 * zz + core, rq)
                part = dot(left_full[0, rows, :], reduced[0], 1, 0)
                for j in range(1, nj):
                    part = part + dot(left_full[j, rows, :], reduced[j], 1, 0)
                if parity == 0:
                    acc[i, zz] = part
                else:
                    sib_send2[i, zz] = part.astype(BF16)
            return inner

        lax.fori_loop(0, n_z, rows_of, 0)
        sib_copies2(i).start()
        return carry

    def forward2(i, carry):
        sib_copies2(i).wait()
        for d in range(1, n_z):
            to = lax.rem(z + d, n_z)
            z_send2[i, d - 1] = (acc[i, to] + sib_recv2[i, to].astype(F32)).astype(BF16)
            z_copies2(i, d).start()
        return carry

    for start in range(0, ni, half):
        lax.fori_loop(start, start + half, relay, 0)
        lax.fori_loop(start, start + half, correlate, 0)
        inverse_factor(gram, eye, inverse, start, half, span, 32)
        if start == 0:
            for d in range(1, n_p):
                pl_copies[d - 1].wait()
            left_full[:, row_block(p, rp), :] = pivot_left[...]
        lax.fori_loop(start, start + half, project, 0)
        lax.fori_loop(start, start + half, forward2, 0)
    finish(c_second, c_chip, c_z, c_own, c_other, c_full, co_s, co_r)

    for i in range(ni):
        rows = pl.ds(i, rq, stride=ni)
        basis[rows, :] = dot(samples[i], -inverse[i], 1, 1, EXACT)
        turned = dot(inverse[i], c_full[i], 1, 0, EXACT).astype(BF16)
        value = dot(target_right[i], turned, 1, 1)
        value = value - acc[i, z] - sib_recv2[i, z].astype(F32)
        for d in range(1, n_z):
            z_copies2(i, d).wait()
            value = value - z_recv2[i, d - 1].astype(F32)
        coefficient[rows, :] = value

    @pl.when(p == owner)
    def _():
        for d in range(1, n_p):
            remote(probe.at[mine()], probe_block, probe_s.at[d - 1], probe_r, peer_p(d)).wait_send()


def per_device(
    n_p, n_q,
    left_factor, right_factor, pivot_left, pivot_right, target_left, target_right, probe, ranks,
):
    ni, nj, order, span = left_factor.shape
    rp = probe.shape[0]
    rq = target_left.shape[0]
    n_z = n_q // 2
    half = ni // 2
    square = (span, span)
    dma = pltpu.SemaphoreType.DMA
    one = dma(())
    z1 = max(n_z - 1, 1)
    p1 = max(n_p - 1, 1)

    def small(wire):
        return [
            pltpu.VMEM((ni,) + square, F32),
            pltpu.VMEM((half,) + square, F32),
            pltpu.VMEM((half,) + square, wire),
            pltpu.VMEM((z1, half) + square, wire),
            pltpu.VMEM((half,) + square, F32),
            pltpu.VMEM((half,) + square, F32),
            pltpu.VMEM((ni,) + square, F32),
        ]

    def exchange():
        return [
            pltpu.VMEM((ni, n_z, rq, span), BF16),
            pltpu.VMEM((ni, n_z, rq, span), BF16),
            pltpu.VMEM((ni, z1, rq, span), BF16),
            pltpu.VMEM((ni, z1, rq, span), BF16),
        ]

    scratch = [
        pltpu.SMEM((ni, nj), jnp.int32),
        pltpu.VMEM((ni, nj, order, span), BF16),
        pltpu.VMEM((ni, nj, order, span), BF16),
        pltpu.VMEM((nj, order, span), BF16),
        pltpu.VMEM((nj, order, span), BF16),
        pltpu.VMEM((rq, span), BF16),
        pltpu.VMEM((ni, nj) + square, F32),
        pltpu.VMEM((nj,) + square, BF16),
        pltpu.VMEM((nj,) + square, F32),
        pltpu.VMEM((p1, nj) + square, F32),
        pltpu.VMEM((nj,) + square, F32),
        *small(F32),
        pltpu.VMEM((ni, n_z, rq, span), F32),
        *exchange(),
        pltpu.VMEM((ni, rq, span), F32),
        pltpu.VMEM((ni, order, span), BF16),
        pltpu.VMEM((ni, nj) + square, F32),
        *small(BF16),
        pltpu.VMEM((ni,) + square, F32),
        pltpu.VMEM((ni,) + square, F32),
        pltpu.VMEM((ni,) + square, F32),
        pltpu.VMEM((nj,) + square, BF16),
        *exchange(),
        dma((3,)),
        dma((p1,)), one,
        dma((p1,)), dma((p1,)), dma((p1,)), dma((p1,)), dma((p1,)), dma((p1,)),
        one, one, dma((z1,)), dma((z1,)), one, one,
        dma((ni,)), dma((ni,)), dma((ni, z1)), dma((ni, z1)),
        dma((ni, z1)), dma((ni, z1)), dma((ni, n_z)), dma((ni, n_z)),
        one, one, dma((z1,)), dma((z1,)), one, one,
        dma((ni,)), dma((ni,)), dma((ni, z1)), dma((ni, z1)),
    ]
    vmem = pl.BlockSpec(memory_space=pltpu.VMEM)
    anywhere = pl.BlockSpec(memory_space=pl.ANY)
    out = jax.ShapeDtypeStruct((rq * ni, span), F32)
    basis, coefficient = pl.pallas_call(
        functools.partial(kernel, n_p, n_q),
        out_shape=(out, out),
        in_specs=[anywhere] * 2 + [vmem] * 5 + [anywhere],
        out_specs=(vmem, vmem),
        scratch_shapes=scratch,
        compiler_params=pltpu.CompilerParams(
            collective_id=0, has_side_effects=True, vmem_limit_bytes=56 * 1024 * 1024
        ),
    )(
        left_factor, right_factor, pivot_left, pivot_right,
        jnp.transpose(target_left, (1, 0, 2)), jnp.transpose(target_right, (1, 0, 2)), probe, ranks,
    )
    basis = jnp.negative(basis)
    coefficient = coefficient * (1.0 / order)
    return basis.reshape(rq, ni, span), coefficient.reshape(rq, ni, span)


def solution(mesh):
    in_specs = (
        P("prow", "pcol", None, None),
        P("prow", "pcol", None, None),
        P("pcol", "prow", None),
        P("pcol", "prow", None),
        P("pcol", "prow", None),
        P("pcol", "prow", None),
        P("prow", None),
        P("prow", "pcol"),
    )
    out_specs = (P("pcol", "prow", None), P("pcol", "prow", None))
    return jax.shard_map(
        functools.partial(per_device, mesh.shape["prow"], mesh.shape["pcol"]),
        mesh=mesh, in_specs=in_specs, out_specs=out_specs, check_vma=False,
    )
```

```python
import functools

import jax
import jax.numpy as jnp
from jax import lax
from jax.experimental import pallas as pl
from jax.experimental.pallas import tpu as pltpu
from jax.sharding import PartitionSpec as P

EXACT = lax.Precision.HIGHEST
MESH = pl.DeviceIdType.MESH
F32 = jnp.float32
BF16 = jnp.bfloat16


def dot(a, b, ca, cb, precision=None):
    return lax.dot_general(
        a, b, (((ca,), (cb,)), ((), ())), precision=precision, preferred_element_type=F32
    )


def inverse_factor(gram_ref, eye_ref, out_ref, start, tiles, span, block):
    row_in_block = lax.broadcasted_iota(jnp.int32, (tiles, block, 1), 1)
    rows = lax.broadcasted_iota(jnp.int32, (tiles, span, span), 1)
    columns = lax.broadcasted_iota(jnp.int32, (tiles, span, span), 2)
    group = slice(start, start + tiles)
    eye_ref[group] = (rows == columns).astype(F32)
    for first in range(0, span, block):
        g = gram_ref[group, first : first + block, :]
        e = eye_ref[group, first : first + block, :]
        for k in range(block):
            column = jnp.broadcast_to(
                g[:, :, first + k : first + k + 1], (tiles, block, span)
            )
            pivot = column[:, k : k + 1, :]
            scale = lax.rsqrt(pivot)
            scale = scale * (1.5 - 0.5 * pivot * scale * scale)
            g_row = g[:, k : k + 1, :] * scale
            e_row = e[:, k : k + 1, :] * scale
            factor = column * scale
            below = row_in_block > k
            here = row_in_block == k
            g = jnp.where(below, g - factor * g_row, jnp.where(here, g_row, g))
            e = jnp.where(below, e - factor * e_row, jnp.where(here, e_row, e))
        out_ref[group, first : first + block, :] = e
        if first + block < span:
            for i in range(tiles):
                gi, ei = g[i], e[i]
                turned = gi.T
                gram_ref[start + i] = gram_ref[start + i] - dot(turned, gi, 1, 0, EXACT)
                eye_ref[start + i] = eye_ref[start + i] - dot(turned, ei, 1, 0, EXACT)


def kernel(
    n_p, n_q,
    left_hbm, right_hbm, pivot_left, pivot_right, target_left, target_right, probe, ranks_hbm,
    basis, coefficient,
    ranks, left, right, left_full, right_full, probe_block, coupling, weights,
    ps_part, ps_recv, ps_sum,
    t_part, t_sib, t_chip, t_z, t_own, t_other, t_full,
    acc, sib_send, sib_recv, up_send, up_recv, down_send, down_recv,
    samples, samples_full, raw,
    c_part, c_sib, c_chip, c_z, c_own, c_other, c_full,
    gram, eye, inverse, reduced,
    sib_send2, sib_recv2, up_send2, up_recv2, down_send2, down_recv2,
    local_sem, probe_s, probe_r, pr_s, pr_r, ps_s, ps_r, pl_s, pl_r,
    ts_s, ts_r, tz_s, tz_r, to_s, to_r,
    ss_s, ss_r, su_s, su_r, sd_s, sd_r,
    gu_s, gu_r, gd_s, gd_r, gs_s, gs_r,
    cs_s, cs_r, cz_s, cz_r, co_s, co_r,
    fs_s, fs_r, fu_s, fu_r, fd_s, fd_r,
):
    p = lax.axis_index("prow")
    q = lax.axis_index("pcol")
    n_z = n_q // 2
    z = q // 2
    c = q % 2
    sibling = (p, q + 1 - 2 * c)
    ni, nj, order, span = left.shape
    rp = probe.shape[0]
    rq = target_left.shape[1]
    half = ni // 2

    def peer_p(d):
        return (lax.rem(p + d, n_p), q)

    def peer_z(d):
        return (p, lax.rem(z + d, n_z) * 2 + c)

    def row_block(index, size):
        return pl.ds(pl.multiple_of(index * size, size), size)

    def remote(src, dst, s, r, where):
        return pltpu.make_async_remote_copy(
            src_ref=src, dst_ref=dst, send_sem=s, recv_sem=r, device_id=where, device_id_type=MESH
        )

    right_copy = pltpu.make_async_copy(right_hbm, right, local_sem.at[0])
    left_copy = pltpu.make_async_copy(left_hbm, left, local_sem.at[1])
    right_copy.start()
    left_copy.start()
    ranks_copy = pltpu.make_async_copy(ranks_hbm, ranks, local_sem.at[2])
    ranks_copy.start()

    barrier = pltpu.get_barrier_semaphore()
    partners = [peer_p(d) for d in range(1, n_p)] + [peer_z(d) for d in range(1, n_z)] + [sibling]
    for partner in partners:
        pl.semaphore_signal(barrier, inc=1, device_id=partner, device_id_type=MESH)
    pl.semaphore_wait(barrier, len(partners))

    owner = (q * rq) // rp

    def mine():
        return pl.ds(pl.multiple_of(lax.rem(q * rq, rp), rq), rq)

    @pl.when(p == owner)
    def _():
        for d in range(1, n_p):
            remote(probe.at[mine()], probe_block, probe_s.at[d - 1], probe_r, peer_p(d)).start()
        probe_block[...] = probe[mine(), :]

    pr_copies = [
        remote(pivot_right, right_full.at[:, row_block(p, rp), :], pr_s.at[d - 1], pr_r.at[d - 1], peer_p(d))
        for d in range(1, n_p)
    ]
    for copy in pr_copies:
        copy.start()
    for j in range(nj):
        ps_part[j] = dot(pivot_left[j], probe[...], 0, 0)
    ps_copies = [
        remote(ps_part, ps_recv.at[d - 1], ps_s.at[d - 1], ps_r.at[d - 1], peer_p(d))
        for d in range(1, n_p)
    ]
    for copy in ps_copies:
        copy.start()
    pl_copies = [
        remote(pivot_left, left_full.at[:, row_block(p, rp), :], pl_s.at[d - 1], pl_r.at[d - 1], peer_p(d))
        for d in range(1, n_p)
    ]
    @pl.when(p != owner)
    def _():
        remote(probe.at[mine()], probe_block, probe_s.at[0], probe_r, peer_p(1)).wait_recv()

    for i in range(ni):
        t_part[i] = dot(target_right[i], probe_block[...], 0, 0)

    def half_of(core):
        return pl.ds(core * half, half)

    t_first = remote(t_part.at[half_of(1 - c)], t_sib, ts_s, ts_r, sibling)
    t_first.start()
    right_copy.wait()

    def couple(rows, chunk_ref):
        def body(n, carry):
            i, j = n // nj, n % nj
            coupling[i, j] += dot(chunk_ref[j], right[i, j, rows, :], 0, 0)
            return carry
        lax.fori_loop(0, ni * nj, body, 0)

    coupling[...] = jnp.zeros_like(coupling)
    couple(row_block(p, rp), pivot_right)

    t_first.wait()
    t_chip[...] = t_part[half_of(c)] + t_sib[...]
    t_second = [
        remote(t_chip, t_z.at[d - 1], tz_s.at[d - 1], tz_r.at[d - 1], peer_z(d)) for d in range(1, n_z)
    ]
    for copy in t_second:
        copy.start()

    for d in range(1, n_p):
        pr_copies[d - 1].wait()
        rows = row_block(lax.rem(p - d + n_p, n_p), rp)
        couple(rows, right_full.at[:, rows, :])
    total = ps_part[...]
    for d in range(1, n_p):
        ps_copies[d - 1].wait()
        total = total + ps_recv[d - 1]
    ps_sum[...] = total
    for copy in pl_copies:
        copy.start()
    left_copy.wait()
    ranks_copy.wait()

    above = (p, lax.rem(z + 1, n_z) * 2 + c)
    beneath = (p, lax.rem(z + n_z - 1, n_z) * 2 + c)

    def chain(siblings, got, u_send, u_recv, d_send, d_recv, us, ur, ds, dr):
        def up(i, t):
            return remote(u_send.at[i, t], u_recv.at[i, t], us.at[i, t], ur.at[i, t], above)

        def down(i, t):
            return remote(d_send.at[i, t], d_recv.at[i, t], ds.at[i, t], dr.at[i, t], beneath)

        def add(i, carry):
            siblings(i).wait()
            for zz in range(n_z):
                acc[i, zz] += got[i, zz].astype(F32)
            return carry

        lax.fori_loop(0, ni, add, 0)

        def one_way(t, i, to, sends, first, copy, out, arrived):
            @pl.when(sends)
            def _():
                @pl.when(first)
                def _():
                    out[i, t] = acc[i, to].astype(BF16)

                @pl.when(jnp.logical_not(first))
                def _():
                    copy(i, t).wait_recv()
                    out[i, t] = (acc[i, to] + arrived[i, t].astype(F32)).astype(BF16)

                copy(i, t).start()

        for t in range(n_z - 1):
            def step(i, carry, t=t):
                top = n_z - 1 - t
                one_way(t, i, top, z < top, z == 0, up, u_send, u_recv)
                one_way(t, i, t, z > t, z == n_z - 1, down, d_send, d_recv)
                return carry

            lax.fori_loop(0, ni, step, 0)

        def finals(i, carry):
            for t in range(n_z - 1):
                @pl.when(z == n_z - 1 - t)
                def _():
                    up(i, t).wait_recv()
                    acc[i, n_z - 1 - t] += u_recv[i, t].astype(F32)

                @pl.when(z == t)
                def _():
                    down(i, t).wait_recv()
                    acc[i, t] += d_recv[i, t].astype(F32)

                @pl.when(z < n_z - 1 - t)
                def _():
                    up(i, t).wait_send()

                @pl.when(z > t)
                def _():
                    down(i, t).wait_send()
            return carry

        lax.fori_loop(0, ni, finals, 0)

    sib_copies = lambda i: remote(sib_send.at[i], sib_recv.at[i], ss_s.at[i], ss_r.at[i], sibling)
    lane = lax.broadcasted_iota(jnp.int32, (span, span), 1)

    def update(i, carry):
        for j in range(nj):
            masked = jnp.where(lane < ranks[i, j], coupling[i, j], 0.0)
            coupling[i, j] = masked
            weights[j] = dot(masked.T, ps_sum[j], 1, 0, EXACT).astype(BF16)

        def rows_of(zz, inner):
            for parity in range(2):
                core = c if parity == 0 else 1 - c
                rows = row_block(2 * zz + core, rq)
                part = dot(left[i, 0, rows, :], weights[0], 1, 0)
                for j in range(1, nj):
                    part = part + dot(left[i, j, rows, :], weights[j], 1, 0)
                if parity == 0:
                    acc[i, zz] = part
                else:
                    sib_send[i, zz] = part.astype(BF16)
            return inner

        lax.fori_loop(0, n_z, rows_of, 0)
        sib_copies(i).start()
        return carry

    lax.fori_loop(0, ni, update, 0)

    chain(sib_copies, sib_recv, up_send, up_recv, down_send, down_recv, su_s, su_r, sd_s, sd_r)

    def finish(second, chip, arrived, own, other, whole, s, r):
        for copy in second:
            copy.wait()
        value = chip[...].astype(F32)
        for d in range(1, n_z):
            value = value + arrived[d - 1].astype(F32)
        own[...] = value
        last = remote(own, other, s, r, sibling)
        last.start()
        last.wait()
        whole[half_of(c)] = own[...]
        whole[half_of(1 - c)] = other[...]

    finish(t_second, t_chip, t_z, t_own, t_other, t_full, to_s, to_r)

    def gather(i, origin, t, s_sem, r_sem, where):
        block = samples_full.at[i, row_block(2 * origin + c, rq), :]
        return remote(block, block, s_sem.at[i, t], r_sem.at[i, t], where)

    def wrap(index):
        return lax.rem(index + n_z, n_z)

    def gather_up(i, t):
        return gather(i, wrap(z - t), t, gu_s, gu_r, above)

    def gather_down(i, t):
        return gather(i, wrap(z + t), t, gd_s, gd_r, beneath)

    def gather_sib(i, origin):
        block = samples_full.at[i, row_block(2 * origin + c, rq), :]
        return remote(block, block, gs_s.at[i, origin], gs_r.at[i, origin], sibling)

    def sample(i, carry):
        value = dot(target_left[i].astype(F32), t_full[i], 1, 0, EXACT)
        value = value - acc[i, z]
        samples[i] = value
        rounded = value.astype(BF16)
        samples_full[i, row_block(q, rq), :] = rounded
        if n_z > 1:
            @pl.when(z < n_z - 1)
            def _():
                gather_up(i, 0).start()

            @pl.when(z > 0)
            def _():
                gather_down(i, 0).start()

        gather_sib(i, z).start()
        c_part[i] = dot(rounded, target_left[i], 0, 0)
        return carry

    lax.fori_loop(0, ni, sample, 0)
    c_first = remote(c_part.at[half_of(1 - c)], c_sib, cs_s, cs_r, sibling)
    c_first.start()

    def relay(t, i):
        @pl.when(z - 1 - t >= 0)
        def _():
            gather_up(i, t).wait_recv()
            if t + 1 < n_z - 1:
                @pl.when(z < n_z - 1)
                def _():
                    gather_up(i, t + 1).start()
            gather_sib(i, wrap(z - 1 - t)).start()

        @pl.when(z + 1 + t < n_z)
        def _():
            gather_down(i, t).wait_recv()
            if t + 1 < n_z - 1:
                @pl.when(z > 0)
                def _():
                    gather_down(i, t + 1).start()
            gather_sib(i, wrap(z + 1 + t)).start()

    def relayed(i, carry):
        for t in range(n_z - 1):
            @pl.when(jnp.logical_and(z < n_z - 1, z - t >= 0))
            def _():
                gather_up(i, t).wait_send()

            @pl.when(jnp.logical_and(z > 0, z + t < n_z))
            def _():
                gather_down(i, t).wait_send()
        return carry

    c_first.wait()
    c_chip[...] = (c_part[half_of(c)] + c_sib[...]).astype(BF16)
    c_second = [
        remote(c_chip, c_z.at[d - 1], cz_s.at[d - 1], cz_r.at[d - 1], peer_z(d)) for d in range(1, n_z)
    ]
    for copy in c_second:
        copy.start()

    def correlate(i, carry):
        for origin in range(n_z):
            gather_sib(i, origin).wait()
        turned = samples_full[i].T
        gram[i] = dot(turned, samples_full[i], 1, 0) * (1.0 / order)
        for j in range(nj):
            raw[i, j] = dot(turned, left[i, j], 1, 0)
        return carry

    sib_copies2 = lambda i: remote(sib_send2.at[i], sib_recv2.at[i], fs_s.at[i], fs_r.at[i], sibling)
    def project(i, carry):
        for j in range(nj):
            turned = dot(inverse[i], raw[i, j], 1, 0, EXACT)
            reduced[j] = dot(coupling[i, j], turned, 1, 1, EXACT).astype(BF16)

        def rows_of(zz, inner):
            for parity in range(2):
                core = c if parity == 0 else 1 - c
                rows = row_block(2 * zz + core, rq)
                part = dot(left_full[0, rows, :], reduced[0], 1, 0)
                for j in range(1, nj):
                    part = part + dot(left_full[j, rows, :], reduced[j], 1, 0)
                if parity == 0:
                    acc[i, zz] = part
                else:
                    sib_send2[i, zz] = part.astype(BF16)
            return inner

        lax.fori_loop(0, n_z, rows_of, 0)
        sib_copies2(i).start()
        return carry

    for t in range(n_z - 1):
        def relay_all(i, carry, t=t):
            relay(t, i)
            return carry

        lax.fori_loop(0, ni, relay_all, 0)
    lax.fori_loop(0, ni, correlate, 0)
    lax.fori_loop(0, ni, relayed, 0)
    inverse_factor(gram, eye, inverse, 0, ni, span, 32)
    for d in range(1, n_p):
        pl_copies[d - 1].wait()
    left_full[:, row_block(p, rp), :] = pivot_left[...]
    lax.fori_loop(0, ni, project, 0)
    chain(sib_copies2, sib_recv2, up_send2, up_recv2, down_send2, down_recv2, fu_s, fu_r, fd_s, fd_r)
    finish(c_second, c_chip, c_z, c_own, c_other, c_full, co_s, co_r)

    for i in range(ni):
        rows = pl.ds(i, rq, stride=ni)
        basis[rows, :] = dot(samples[i], -inverse[i], 1, 1, EXACT)
        turned = dot(inverse[i], c_full[i], 1, 0, EXACT).astype(BF16)
        value = dot(target_right[i], turned, 1, 1)
        value = value - acc[i, z]
        coefficient[rows, :] = value

    @pl.when(p == owner)
    def _():
        for d in range(1, n_p):
            remote(probe.at[mine()], probe_block, probe_s.at[d - 1], probe_r, peer_p(d)).wait_send()


def per_device(
    n_p, n_q,
    left_factor, right_factor, pivot_left, pivot_right, target_left, target_right, probe, ranks,
):
    ni, nj, order, span = left_factor.shape
    rp = probe.shape[0]
    rq = target_left.shape[0]
    n_z = n_q // 2
    half = ni // 2
    square = (span, span)
    dma = pltpu.SemaphoreType.DMA
    one = dma(())
    z1 = max(n_z - 1, 1)
    p1 = max(n_p - 1, 1)

    def small(wire):
        return [
            pltpu.VMEM((ni,) + square, F32),
            pltpu.VMEM((half,) + square, F32),
            pltpu.VMEM((half,) + square, wire),
            pltpu.VMEM((z1, half) + square, wire),
            pltpu.VMEM((half,) + square, F32),
            pltpu.VMEM((half,) + square, F32),
            pltpu.VMEM((ni,) + square, F32),
        ]

    def exchange():
        return [
            pltpu.VMEM((ni, n_z, rq, span), BF16),
            pltpu.VMEM((ni, n_z, rq, span), BF16),
            pltpu.VMEM((ni, z1, rq, span), BF16),
            pltpu.VMEM((ni, z1, rq, span), BF16),
            pltpu.VMEM((ni, z1, rq, span), BF16),
            pltpu.VMEM((ni, z1, rq, span), BF16),
        ]

    scratch = [
        pltpu.SMEM((ni, nj), jnp.int32),
        pltpu.VMEM((ni, nj, order, span), BF16),
        pltpu.VMEM((ni, nj, order, span), BF16),
        pltpu.VMEM((nj, order, span), BF16),
        pltpu.VMEM((nj, order, span), BF16),
        pltpu.VMEM((rq, span), BF16),
        pltpu.VMEM((ni, nj) + square, F32),
        pltpu.VMEM((nj,) + square, BF16),
        pltpu.VMEM((nj,) + square, F32),
        pltpu.VMEM((p1, nj) + square, F32),
        pltpu.VMEM((nj,) + square, F32),
        *small(F32),
        pltpu.VMEM((ni, n_z, rq, span), F32),
        *exchange(),
        pltpu.VMEM((ni, rq, span), F32),
        pltpu.VMEM((ni, order, span), BF16),
        pltpu.VMEM((ni, nj) + square, F32),
        *small(BF16),
        pltpu.VMEM((ni,) + square, F32),
        pltpu.VMEM((ni,) + square, F32),
        pltpu.VMEM((ni,) + square, F32),
        pltpu.VMEM((nj,) + square, BF16),
        *exchange(),
        dma((3,)),
        dma((p1,)), one,
        dma((p1,)), dma((p1,)), dma((p1,)), dma((p1,)), dma((p1,)), dma((p1,)),
        one, one, dma((z1,)), dma((z1,)), one, one,
        dma((ni,)), dma((ni,)), dma((ni, z1)), dma((ni, z1)), dma((ni, z1)), dma((ni, z1)),
        dma((ni, z1)), dma((ni, z1)), dma((ni, z1)), dma((ni, z1)), dma((ni, n_z)), dma((ni, n_z)),
        one, one, dma((z1,)), dma((z1,)), one, one,
        dma((ni,)), dma((ni,)), dma((ni, z1)), dma((ni, z1)), dma((ni, z1)), dma((ni, z1)),
    ]
    vmem = pl.BlockSpec(memory_space=pltpu.VMEM)
    anywhere = pl.BlockSpec(memory_space=pl.ANY)
    out = jax.ShapeDtypeStruct((rq * ni, span), F32)
    basis, coefficient = pl.pallas_call(
        functools.partial(kernel, n_p, n_q),
        out_shape=(out, out),
        in_specs=[anywhere] * 2 + [vmem] * 5 + [anywhere],
        out_specs=(vmem, vmem),
        scratch_shapes=scratch,
        compiler_params=pltpu.CompilerParams(
            collective_id=0, has_side_effects=True, vmem_limit_bytes=56 * 1024 * 1024
        ),
    )(
        left_factor, right_factor, pivot_left, pivot_right,
        jnp.transpose(target_left, (1, 0, 2)), jnp.transpose(target_right, (1, 0, 2)), probe, ranks,
    )
    basis = jnp.negative(basis)
    coefficient = coefficient * (1.0 / order)
    return basis.reshape(rq, ni, span), coefficient.reshape(rq, ni, span)


def solution(mesh):
    in_specs = (
        P("prow", "pcol", None, None),
        P("prow", "pcol", None, None),
        P("pcol", "prow", None),
        P("pcol", "prow", None),
        P("pcol", "prow", None),
        P("pcol", "prow", None),
        P("prow", None),
        P("prow", "pcol"),
    )
    out_specs = (P("pcol", "prow", None), P("pcol", "prow", None))
    return jax.shard_map(
        functools.partial(per_device, mesh.shape["prow"], mesh.shape["pcol"]),
        mesh=mesh, in_specs=in_specs, out_specs=out_specs, check_vma=False,
    )
```

```python
import functools

import jax
import jax.numpy as jnp
from jax import lax
from jax.experimental import pallas as pl
from jax.experimental.pallas import tpu as pltpu
from jax.sharding import PartitionSpec as P

EXACT = lax.Precision.HIGHEST
MESH = pl.DeviceIdType.MESH
F32 = jnp.float32
BF16 = jnp.bfloat16


def dot(a, b, ca, cb, precision=None):
    return lax.dot_general(
        a, b, (((ca,), (cb,)), ((), ())), precision=precision, preferred_element_type=F32
    )


def inverse_factor(gram_ref, eye_ref, out_ref, start, tiles, span, block):
    row_in_block = lax.broadcasted_iota(jnp.int32, (tiles, block, 1), 1)
    rows = lax.broadcasted_iota(jnp.int32, (tiles, span, span), 1)
    columns = lax.broadcasted_iota(jnp.int32, (tiles, span, span), 2)
    group = slice(start, start + tiles)
    eye_ref[group] = (rows == columns).astype(F32)
    for first in range(0, span, block):
        g = gram_ref[group, first : first + block, :]
        e = eye_ref[group, first : first + block, :]
        for k in range(block):
            column = jnp.broadcast_to(
                g[:, :, first + k : first + k + 1], (tiles, block, span)
            )
            pivot = column[:, k : k + 1, :]
            scale = lax.rsqrt(pivot)
            scale = scale * (1.5 - 0.5 * pivot * scale * scale)
            g_row = g[:, k : k + 1, :] * scale
            e_row = e[:, k : k + 1, :] * scale
            factor = column * scale
            below = row_in_block > k
            here = row_in_block == k
            g = jnp.where(below, g - factor * g_row, jnp.where(here, g_row, g))
            e = jnp.where(below, e - factor * e_row, jnp.where(here, e_row, e))
        out_ref[group, first : first + block, :] = e
        if first + block < span:
            for i in range(tiles):
                gi, ei = g[i], e[i]
                turned = gi.T
                gram_ref[start + i] = gram_ref[start + i] - dot(turned, gi, 1, 0, EXACT)
                eye_ref[start + i] = eye_ref[start + i] - dot(turned, ei, 1, 0, EXACT)


def kernel(
    n_p, n_q,
    left_hbm, right_hbm, pivot_left, pivot_right, target_left, target_right, probe, ranks_hbm,
    basis, coefficient,
    ranks, left, right, left_full, right_full, probe_block, coupling, weights,
    ps_part, ps_recv, ps_sum,
    t_part, t_sib, t_chip, t_z, t_own, t_other, t_full,
    acc, sib_send, sib_recv, z_send, z_recv,
    samples, samples_full, raw,
    c_part, c_sib, c_chip, c_z, c_own, c_other, c_full,
    gram, eye, inverse, reduced,
    sib_send2, sib_recv2, z_send2, z_recv2,
    local_sem, probe_s, probe_r, pr_s, pr_r, ps_s, ps_r, pl_s, pl_r,
    ts_s, ts_r, tz_s, tz_r, to_s, to_r,
    ss_s, ss_r, sz_s, sz_r,
    gz_s, gz_r, gs_s, gs_r,
    cs_s, cs_r, cz_s, cz_r, co_s, co_r,
    fs_s, fs_r, fz_s, fz_r,
):
    p = lax.axis_index("prow")
    q = lax.axis_index("pcol")
    n_z = n_q // 2
    z = q // 2
    c = q % 2
    sibling = (p, q + 1 - 2 * c)
    ni, nj, order, span = left.shape
    rp = probe.shape[0]
    rq = target_left.shape[1]
    half = ni // 2

    def peer_p(d):
        return (lax.rem(p + d, n_p), q)

    def peer_z(d):
        return (p, lax.rem(z + d, n_z) * 2 + c)

    def row_block(index, size):
        return pl.ds(pl.multiple_of(index * size, size), size)

    def remote(src, dst, s, r, where):
        return pltpu.make_async_remote_copy(
            src_ref=src, dst_ref=dst, send_sem=s, recv_sem=r, device_id=where, device_id_type=MESH
        )

    right_copy = pltpu.make_async_copy(right_hbm, right, local_sem.at[0])
    left_copy = pltpu.make_async_copy(left_hbm, left, local_sem.at[1])
    right_copy.start()
    left_copy.start()
    ranks_copy = pltpu.make_async_copy(ranks_hbm, ranks, local_sem.at[2])
    ranks_copy.start()

    barrier = pltpu.get_barrier_semaphore()
    partners = [peer_p(d) for d in range(1, n_p)] + [peer_z(d) for d in range(1, n_z)] + [sibling]
    for partner in partners:
        pl.semaphore_signal(barrier, inc=1, device_id=partner, device_id_type=MESH)
    pl.semaphore_wait(barrier, len(partners))

    owner = (q * rq) // rp

    def mine():
        return pl.ds(pl.multiple_of(lax.rem(q * rq, rp), rq), rq)

    @pl.when(p == owner)
    def _():
        for d in range(1, n_p):
            remote(probe.at[mine()], probe_block, probe_s.at[d - 1], probe_r, peer_p(d)).start()
        probe_block[...] = probe[mine(), :]

    pr_copies = [
        remote(pivot_right, right_full.at[:, row_block(p, rp), :], pr_s.at[d - 1], pr_r.at[d - 1], peer_p(d))
        for d in range(1, n_p)
    ]
    for copy in pr_copies:
        copy.start()
    for j in range(nj):
        ps_part[j] = dot(pivot_left[j], probe[...], 0, 0)
    ps_copies = [
        remote(ps_part, ps_recv.at[d - 1], ps_s.at[d - 1], ps_r.at[d - 1], peer_p(d))
        for d in range(1, n_p)
    ]
    for copy in ps_copies:
        copy.start()
    pl_copies = [
        remote(pivot_left, left_full.at[:, row_block(p, rp), :], pl_s.at[d - 1], pl_r.at[d - 1], peer_p(d))
        for d in range(1, n_p)
    ]
    @pl.when(p != owner)
    def _():
        remote(probe.at[mine()], probe_block, probe_s.at[0], probe_r, peer_p(1)).wait_recv()

    for i in range(ni):
        t_part[i] = dot(target_right[i], probe_block[...], 0, 0)

    def half_of(core):
        return pl.ds(core * half, half)

    t_first = remote(t_part.at[half_of(1 - c)], t_sib, ts_s, ts_r, sibling)
    t_first.start()
    right_copy.wait()

    def couple(rows, chunk_ref):
        def body(n, carry):
            i, j = n // nj, n % nj
            coupling[i, j] += dot(chunk_ref[j], right[i, j, rows, :], 0, 0)
            return carry
        lax.fori_loop(0, ni * nj, body, 0, unroll=True)

    coupling[...] = jnp.zeros_like(coupling)
    couple(row_block(p, rp), pivot_right)

    t_first.wait()
    t_chip[...] = t_part[half_of(c)] + t_sib[...]
    t_second = [
        remote(t_chip, t_z.at[d - 1], tz_s.at[d - 1], tz_r.at[d - 1], peer_z(d)) for d in range(1, n_z)
    ]
    for copy in t_second:
        copy.start()

    for d in range(1, n_p):
        pr_copies[d - 1].wait()
        rows = row_block(lax.rem(p - d + n_p, n_p), rp)
        couple(rows, right_full.at[:, rows, :])
    total = ps_part[...]
    for d in range(1, n_p):
        ps_copies[d - 1].wait()
        total = total + ps_recv[d - 1]
    ps_sum[...] = total
    for copy in pl_copies:
        copy.start()
    left_copy.wait()
    ranks_copy.wait()

    sib_copies = lambda i: remote(sib_send.at[i], sib_recv.at[i], ss_s.at[i], ss_r.at[i], sibling)
    z_copies = lambda i, d: remote(
        z_send.at[i, d - 1], z_recv.at[i, d - 1], sz_s.at[i, d - 1], sz_r.at[i, d - 1], peer_z(d)
    )
    lane = lax.broadcasted_iota(jnp.int32, (span, span), 1)

    for i in range(ni):
        for j in range(nj):
            masked = jnp.where(lane < ranks[i, j], coupling[i, j], 0.0)
            coupling[i, j] = masked
            weights[i, j] = dot(masked.T, ps_sum[j], 1, 0, EXACT).astype(BF16)

    def update(i, carry):
        def rows_of(zz, inner):
            for parity in range(2):
                core = c if parity == 0 else 1 - c
                rows = row_block(2 * zz + core, rq)
                part = dot(left[i, 0, rows, :], weights[i, 0], 1, 0)
                for j in range(1, nj):
                    part = part + dot(left[i, j, rows, :], weights[i, j], 1, 0)
                if parity == 0:
                    acc[i, zz] = part
                else:
                    sib_send[i, zz] = part.astype(BF16)
            return inner

        lax.fori_loop(0, n_z, rows_of, 0, unroll=True)
        sib_copies(i).start()
        return carry

    lax.fori_loop(0, ni, update, 0)

    def forward(i, carry):
        sib_copies(i).wait()
        for d in range(1, n_z):
            to = lax.rem(z + d, n_z)
            z_send[i, d - 1] = (acc[i, to] + sib_recv[i, to].astype(F32)).astype(BF16)
            z_copies(i, d).start()
        return carry

    def sent(i, carry):
        for d in range(1, n_z):
            z_copies(i, d).wait_send()
        return carry

    lax.fori_loop(0, half, forward, 0)

    def finish(second, chip, arrived, own, other, whole, s, r):
        for copy in second:
            copy.wait()
        value = chip[...].astype(F32)
        for d in range(1, n_z):
            value = value + arrived[d - 1].astype(F32)
        own[...] = value
        last = remote(own, other, s, r, sibling)
        last.start()
        last.wait()
        whole[half_of(c)] = own[...]
        whole[half_of(1 - c)] = other[...]

    finish(t_second, t_chip, t_z, t_own, t_other, t_full, to_s, to_r)
    lax.fori_loop(0, half, sent, 0)
    lax.fori_loop(half, ni, forward, 0)

    gather_z = lambda i, d: remote(
        samples_full.at[i, row_block(q, rq), :], samples_full.at[i, row_block(q, rq), :],
        gz_s.at[i, d - 1], gz_r.at[i, d - 1], peer_z(d),
    )

    def gather_sib(i, d):
        rows = row_block(2 * lax.rem(z - d + n_z, n_z) + c, rq)
        block = samples_full.at[i, rows, :]
        return remote(block, block, gs_s.at[i, d], gs_r.at[i, d], sibling)

    def sample(i, carry):
        value = dot(target_left[i].astype(F32), t_full[i], 1, 0, EXACT)
        value = value - acc[i, z] - sib_recv[i, z].astype(F32)
        for d in range(1, n_z):
            z_copies(i, d).wait_recv()
            value = value - z_recv[i, d - 1].astype(F32)
        samples[i] = value
        rounded = value.astype(BF16)
        samples_full[i, row_block(q, rq), :] = rounded
        for d in range(1, n_z):
            gather_z(i, d).start()
        gather_sib(i, 0).start()
        c_part[i] = dot(rounded, target_left[i], 0, 0)
        return carry

    lax.fori_loop(0, ni, sample, 0)
    lax.fori_loop(half, ni, sent, 0)
    c_first = remote(c_part.at[half_of(1 - c)], c_sib, cs_s, cs_r, sibling)
    c_first.start()

    def relay(i, carry):
        for d in range(1, n_z):
            gather_z(i, d).wait()
            gather_sib(i, d).start()
        return carry

    c_first.wait()
    c_chip[...] = (c_part[half_of(c)] + c_sib[...]).astype(BF16)
    c_second = [
        remote(c_chip, c_z.at[d - 1], cz_s.at[d - 1], cz_r.at[d - 1], peer_z(d)) for d in range(1, n_z)
    ]
    for copy in c_second:
        copy.start()

    def correlate(i, carry):
        for d in range(n_z):
            gather_sib(i, d).wait()
        turned = samples_full[i].T
        gram[i] = dot(turned, samples_full[i], 1, 0) * (1.0 / order)
        for j in range(nj):
            raw[i, j] = dot(turned, left[i, j], 1, 0)
        return carry

    sib_copies2 = lambda i: remote(sib_send2.at[i], sib_recv2.at[i], fs_s.at[i], fs_r.at[i], sibling)
    z_copies2 = lambda i, d: remote(
        z_send2.at[i, d - 1], z_recv2.at[i, d - 1], fz_s.at[i, d - 1], fz_r.at[i, d - 1], peer_z(d)
    )

    def reduce(start):
        pairs = [(i, j) for i in range(start, start + half) for j in range(nj)]
        turned = [dot(inverse[i], raw[i, j], 1, 0, EXACT) for i, j in pairs]
        for (i, j), value in zip(pairs, turned):
            reduced[i, j] = dot(coupling[i, j], value, 1, 1, EXACT).astype(BF16)

    def project(i, carry):
        def rows_of(zz, inner):
            for parity in range(2):
                core = c if parity == 0 else 1 - c
                rows = row_block(2 * zz + core, rq)
                part = dot(left_full[0, rows, :], reduced[i, 0], 1, 0)
                for j in range(1, nj):
                    part = part + dot(left_full[j, rows, :], reduced[i, j], 1, 0)
                if parity == 0:
                    acc[i, zz] = part
                else:
                    sib_send2[i, zz] = part.astype(BF16)
            return inner

        lax.fori_loop(0, n_z, rows_of, 0, unroll=True)
        sib_copies2(i).start()
        return carry

    def forward2(i, carry):
        sib_copies2(i).wait()
        for d in range(1, n_z):
            to = lax.rem(z + d, n_z)
            z_send2[i, d - 1] = (acc[i, to] + sib_recv2[i, to].astype(F32)).astype(BF16)
            z_copies2(i, d).start()
        return carry

    for start in range(0, ni, half):
        lax.fori_loop(start, start + half, relay, 0)
        lax.fori_loop(start, start + half, correlate, 0, unroll=True)
        inverse_factor(gram, eye, inverse, start, half, span, 32)
        if start == 0:
            for d in range(1, n_p):
                pl_copies[d - 1].wait()
            left_full[:, row_block(p, rp), :] = pivot_left[...]
        reduce(start)
        lax.fori_loop(start, start + half, project, 0)
        lax.fori_loop(start, start + half, forward2, 0)
    finish(c_second, c_chip, c_z, c_own, c_other, c_full, co_s, co_r)

    for i in range(ni):
        rows = pl.ds(i, rq, stride=ni)
        basis[rows, :] = dot(samples[i], -inverse[i], 1, 1, EXACT)
        turned = dot(inverse[i], c_full[i], 1, 0, EXACT).astype(BF16)
        value = dot(target_right[i], turned, 1, 1)
        value = value - acc[i, z] - sib_recv2[i, z].astype(F32)
        for d in range(1, n_z):
            z_copies2(i, d).wait()
            value = value - z_recv2[i, d - 1].astype(F32)
        coefficient[rows, :] = value

    @pl.when(p == owner)
    def _():
        for d in range(1, n_p):
            remote(probe.at[mine()], probe_block, probe_s.at[d - 1], probe_r, peer_p(d)).wait_send()


def per_device(
    n_p, n_q,
    left_factor, right_factor, pivot_left, pivot_right, target_left, target_right, probe, ranks,
):
    ni, nj, order, span = left_factor.shape
    rp = probe.shape[0]
    rq = target_left.shape[0]
    n_z = n_q // 2
    half = ni // 2
    square = (span, span)
    dma = pltpu.SemaphoreType.DMA
    one = dma(())
    z1 = max(n_z - 1, 1)
    p1 = max(n_p - 1, 1)

    def small(wire):
        return [
            pltpu.VMEM((ni,) + square, F32),
            pltpu.VMEM((half,) + square, F32),
            pltpu.VMEM((half,) + square, wire),
            pltpu.VMEM((z1, half) + square, wire),
            pltpu.VMEM((half,) + square, F32),
            pltpu.VMEM((half,) + square, F32),
            pltpu.VMEM((ni,) + square, F32),
        ]

    def exchange():
        return [
            pltpu.VMEM((ni, n_z, rq, span), BF16),
            pltpu.VMEM((ni, n_z, rq, span), BF16),
            pltpu.VMEM((ni, z1, rq, span), BF16),
            pltpu.VMEM((ni, z1, rq, span), BF16),
        ]

    scratch = [
        pltpu.SMEM((ni, nj), jnp.int32),
        pltpu.VMEM((ni, nj, order, span), BF16),
        pltpu.VMEM((ni, nj, order, span), BF16),
        pltpu.VMEM((nj, order, span), BF16),
        pltpu.VMEM((nj, order, span), BF16),
        pltpu.VMEM((rq, span), BF16),
        pltpu.VMEM((ni, nj) + square, F32),
        pltpu.VMEM((ni, nj) + square, BF16),
        pltpu.VMEM((nj,) + square, F32),
        pltpu.VMEM((p1, nj) + square, F32),
        pltpu.VMEM((nj,) + square, F32),
        *small(F32),
        pltpu.VMEM((ni, n_z, rq, span), F32),
        *exchange(),
        pltpu.VMEM((ni, rq, span), F32),
        pltpu.VMEM((ni, order, span), BF16),
        pltpu.VMEM((ni, nj) + square, F32),
        *small(BF16),
        pltpu.VMEM((ni,) + square, F32),
        pltpu.VMEM((ni,) + square, F32),
        pltpu.VMEM((ni,) + square, F32),
        pltpu.VMEM((ni, nj) + square, BF16),
        *exchange(),
        dma((3,)),
        dma((p1,)), one,
        dma((p1,)), dma((p1,)), dma((p1,)), dma((p1,)), dma((p1,)), dma((p1,)),
        one, one, dma((z1,)), dma((z1,)), one, one,
        dma((ni,)), dma((ni,)), dma((ni, z1)), dma((ni, z1)),
        dma((ni, z1)), dma((ni, z1)), dma((ni, n_z)), dma((ni, n_z)),
        one, one, dma((z1,)), dma((z1,)), one, one,
        dma((ni,)), dma((ni,)), dma((ni, z1)), dma((ni, z1)),
    ]
    vmem = pl.BlockSpec(memory_space=pltpu.VMEM)
    anywhere = pl.BlockSpec(memory_space=pl.ANY)
    out = jax.ShapeDtypeStruct((rq * ni, span), F32)
    basis, coefficient = pl.pallas_call(
        functools.partial(kernel, n_p, n_q),
        out_shape=(out, out),
        in_specs=[anywhere] * 2 + [vmem] * 5 + [anywhere],
        out_specs=(vmem, vmem),
        scratch_shapes=scratch,
        compiler_params=pltpu.CompilerParams(
            collective_id=0, has_side_effects=True, vmem_limit_bytes=56 * 1024 * 1024
        ),
    )(
        left_factor, right_factor, pivot_left, pivot_right,
        jnp.transpose(target_left, (1, 0, 2)), jnp.transpose(target_right, (1, 0, 2)), probe, ranks,
    )
    basis = jnp.negative(basis)
    coefficient = coefficient * (1.0 / order)
    return basis.reshape(rq, ni, span), coefficient.reshape(rq, ni, span)


def solution(mesh):
    in_specs = (
        P("prow", "pcol", None, None),
        P("prow", "pcol", None, None),
        P("pcol", "prow", None),
        P("pcol", "prow", None),
        P("pcol", "prow", None),
        P("pcol", "prow", None),
        P("prow", None),
        P("prow", "pcol"),
    )
    out_specs = (P("pcol", "prow", None), P("pcol", "prow", None))
    return jax.shard_map(
        functools.partial(per_device, mesh.shape["prow"], mesh.shape["pcol"]),
        mesh=mesh, in_specs=in_specs, out_specs=out_specs, check_vma=False,
    )
```
